32 devices in a mesh: dp: 8 (over y, x, core), tensor: 4 (over z).
Axes of the slice: x: 2, y: 2, z: 4, core: 2. Of those that a mesh axis runs over, the one named last changes fastest.
Arguments:
- tokens: bfloat16 [512, 4096], P(('dp', 'tensor')), parts along dimension 0, may hold values from -6 to 6
- gate_act: bfloat16 [512, 5120], P('dp', 'tensor'), parts along dimension 0, may hold values from -6 to 6
- up_act: bfloat16 [512, 5120], P('dp', 'tensor'), parts along dimension 0, may hold values from -6 to 6
- down_weight: bfloat16 [5120, 4096], P('tensor'), may hold values from -0.078125 to 0.078125
- norm_gain: float32 [4096], replicated, may hold values from 0.25 to 1.75
Outputs:
- residual_out: bfloat16 [512, 4096], P(('dp', 'tensor')), parts along dimension 0
- next_rows: bfloat16 [512, 4096], P('dp'), parts along dimension 0
- next_scale: float32 [512], P('dp'), parts along dimension 0
The draws below stay inside these ranges and needn't reach their ends.
There are 8 independent parts, one for each index of `dp`. The reference program is written for one: setup_inputs(seed, part) draws one part's arguments, and reference() takes and returns one part's arrays. A program takes and returns all parts, laid end to end along the dimension named above; an argument that names none is the same for every part. Nothing has to cross between parts.
All inputs are finite; a program needn't handle non-finite values. Where the reference program divides by a largest or mean magnitude, that divisor is 1e-20 or more.
Results may differ from the reference program's by a relative error of at most 0.009.
Values may be sent and summed in bfloat16 or wider, within the bound.
No kernel may reach another device: no remote copies, remote signals or barrier semaphores. Data moves between devices by JAX's collectives and lax.ppermute only.
A program may use at most 64 MiB of HBM per device.

```python
import jax
import jax.numpy as jnp
from jax import lax

D = 4096
FF_DEV = 1280
TOKENS = 64
FF = 5120
N_TENSOR = 4


def level_of(stream_key, extent, shards, low, largest):
    factor_of, own = 1.0, jax.random.fold_in(stream_key, 6)
    for position, shards_of in shards:
        heights = jnp.exp(jax.random.uniform(jax.random.fold_in(own, position), (shards_of,), jnp.float32, low / len(shards), largest / len(shards)))
        factor_of = factor_of * jnp.repeat(heights, extent[position] // shards_of).reshape([-1 if axis == position else 1 for axis in range(len(extent))])
    return factor_of


def gaussian(own_key, extent, scale, limit, cuts=(), dtype=jnp.bfloat16):
    entries = scale * jax.random.normal(own_key, extent, jnp.float32)
    if cuts:
        entries = entries * level_of(own_key, extent, cuts, -0.22, 0.18)
    return jnp.clip(entries, -limit, limit).astype(dtype)


def setup_inputs(seed: int = 0, part: int = 0) -> dict:
    keys = jax.random.split(jax.random.key(seed), 6)
    part_keys = jax.random.split(jax.random.fold_in(keys[5], part), 6)
    return {
        "tokens": gaussian(part_keys[0], (TOKENS, D), 1.0, 6.0, ((0, 4),)),
        "gate_act": gaussian(part_keys[1], (TOKENS, FF), 1.0, 6.0, ((1, 4),)),
        "up_act": gaussian(part_keys[2], (TOKENS, FF), 1.0, 6.0, ((1, 4),)),
        "down_weight": gaussian(keys[3], (FF, D), FF ** -0.5, 0.078125, ((0, 4),)),
        "norm_gain": jnp.clip(1.0 + 0.15 * jax.random.normal(keys[4], (D,), jnp.float32), 0.25, 1.75),
    }


def reference(tokens, gate_act, up_act, down_weight, norm_gain):
    hidden = (jax.nn.silu(gate_act.astype(jnp.float32)) * up_act.astype(jnp.float32)).astype(jnp.bfloat16)
    total = jnp.zeros((tokens.shape[0], tokens.shape[1]), jnp.float32)
    for group in range(N_TENSOR):
        part_hidden = hidden[:, group * FF_DEV:(group + 1) * FF_DEV]
        part_down = down_weight[group * FF_DEV:(group + 1) * FF_DEV, :]
        product = jnp.dot(part_hidden, part_down, preferred_element_type=jnp.float32)
        rounded = lax.optimization_barrier(product.astype(jnp.bfloat16))
        total = total + rounded.astype(jnp.float32)
    residual = tokens.astype(jnp.float32) + total
    mean_square = lax.optimization_barrier(jnp.mean(residual * residual, axis=1, keepdims=True))
    normed = residual * lax.rsqrt(mean_square + 1e-05) * norm_gain[None, :]
    next_scale = lax.optimization_barrier(jnp.max(jnp.abs(normed), axis=1))
    next_rows = (normed / next_scale[:, None]).astype(jnp.bfloat16)
    return (residual.astype(jnp.bfloat16), next_rows, next_scale)
```

```python
import functools

import jax
import jax.numpy as jnp
from jax import lax
from jax.experimental import pallas as pl
from jax.experimental.pallas import tpu as pltpu
from jax.sharding import PartitionSpec as P

F32, BF16 = jnp.float32, jnp.bfloat16
SHARES = (1,1)
VMEM_LIMIT = 32 * 1024 * 1024


def spans_of(half):
    whole, at, spans = sum(SHARES), 0, []
    for share in SHARES:
        width = half * share // whole // 128 * 128
        spans.append([at, width])
        at += width
    spans[-1][1] = half - spans[-1][0]
    return [tuple(span) for span in spans]


def project_kernel(n, half, spans, keep, gated, *refs):
    k = len(spans)
    if gated:
        gate_hbm, up_hbm, tokens_hbm, weight_ref, *refs = refs
    else:
        hidden_ref, tokens_hbm, weight_ref, *refs = refs
    outs, refs = refs[:k], refs[k:]
    if gated:
        hidden_ref, gate_ref, up_ref, *refs = refs
    tokens_ref, *refs = refs
    buffers, sem = refs[:k], refs[k]
    me = lax.axis_index("tensor")
    side = lax.rem(me, 2) if keep else 1 - lax.rem(me, 2)

    def fetch(source, target, i):
        copy = pltpu.make_async_copy(source, target, sem.at[i])
        copy.start()
        return copy

    if gated:
        gating = [fetch(gate_hbm, gate_ref, k + 1), fetch(up_hbm, up_ref, k + 2)]
    copies = []
    for i, (at, width) in enumerate(spans):
        cols = pl.ds(pl.multiple_of(side * half + at, 128), width)
        copies.append(fetch(weight_ref.at[:, cols], buffers[i], i))
        if i == 0:
            adding = fetch(tokens_hbm, tokens_ref, k)
    if gated:
        for copy in gating:
            copy.wait()
        gate = gate_ref[...].astype(F32)
        hidden_ref[...] = (gate / (1.0 + jnp.exp(-gate)) * up_ref[...].astype(F32)).astype(BF16)
    rows = tokens_ref.shape[0]
    for i, (at, width) in enumerate(spans):
        copies[i].wait()
        if i == 0:
            adding.wait()
        cols = pl.ds(pl.multiple_of(side * half + at, 128), width)
        own = jnp.concatenate([tokens_ref[:, cols].astype(F32)] * n, axis=0)
        owner = lax.broadcasted_iota(jnp.int32, own.shape, 0) // rows
        product = jnp.dot(hidden_ref[...], buffers[i][...], preferred_element_type=F32)
        outs[i][...] = (product + jnp.where(owner == me, own, 0.0)).astype(BF16)


def project(n, spans, keep, gated, ins, tokens, weight):
    depth, width = weight.shape
    rows = tokens.shape[0] * n
    vmem, hbm = pl.BlockSpec(memory_space=pltpu.VMEM), pl.BlockSpec(memory_space=pltpu.HBM)
    shapes = [jax.ShapeDtypeStruct((rows, w), BF16) for _, w in spans]
    scratch = [pltpu.VMEM(tokens.shape, BF16)]
    if gated:
        shapes.append(jax.ShapeDtypeStruct((rows, depth), BF16))
        scratch = [pltpu.VMEM((rows, depth), BF16)] * 2 + scratch
    columns = sum(w for _, w in spans)
    pinned = [*(ins if gated else ()), tokens, weight]
    pinned = [pltpu.with_memory_space_constraint(x, pltpu.HBM) for x in pinned]
    return pl.pallas_call(
        functools.partial(project_kernel, n, width // 2, spans, keep, gated),
        out_shape=shapes,
        in_specs=[hbm if gated else vmem] * len(ins) + [hbm, hbm],
        out_specs=[vmem] * len(shapes),
        scratch_shapes=scratch
        + [pltpu.VMEM((depth, w), BF16) for _, w in spans]
        + [pltpu.SemaphoreType.DMA((len(spans) + 3,))],
        compiler_params=pltpu.CompilerParams(vmem_limit_bytes=VMEM_LIMIT),
        cost_estimate=pl.CostEstimate(
            flops=2 * rows * depth * columns,
            bytes_accessed=2 * depth * columns,
            transcendentals=0,
        ),
    )(*(() if gated else ins), *pinned)


def norm_kernel(half, spans, *refs):
    k = len(spans)
    own, other = refs[:k], refs[k : 2 * k]
    gain_ref, residual_ref, rows_ref, scale_ref, scaled_ref = refs[2 * k :]
    me = lax.axis_index("tensor")
    side = lax.rem(me, 2)
    mine = pl.ds(pl.multiple_of(me * residual_ref.shape[0], 16), residual_ref.shape[0])
    squares, largest = 0.0, 0.0
    for base, pieces in ((side * half, own), ((1 - side) * half, other)):
        for (at, width), piece in zip(spans, pieces):
            cols = pl.ds(pl.multiple_of(base + at, 128), width)
            residual_ref[:, cols] = piece[mine, :]
            residual = piece[...].astype(F32)
            scaled = residual * gain_ref[:, cols]
            scaled_ref[:, cols] = scaled
            squares += jnp.sum(residual * residual, axis=1, keepdims=True)
            largest = jnp.maximum(largest, jnp.max(jnp.abs(scaled), axis=1, keepdims=True))
    rows_ref[...] = (scaled_ref[...] * (1.0 / largest)).astype(BF16)
    scale_ref[...] = (largest * lax.rsqrt(squares * (0.5 / half) + 1e-05)).reshape(-1)


def norm(rows, spans, own, other, gain):
    count, width = own[0].shape[0], gain.shape[0]
    vmem = pl.BlockSpec(memory_space=pltpu.VMEM)
    return pl.pallas_call(
        functools.partial(norm_kernel, width // 2, spans),
        out_shape=[
            jax.ShapeDtypeStruct((rows, width), BF16),
            jax.ShapeDtypeStruct((count, width), BF16),
            jax.ShapeDtypeStruct((count,), F32),
        ],
        in_specs=[vmem] * (2 * len(spans) + 1),
        out_specs=[vmem] * 3,
        scratch_shapes=[pltpu.VMEM((count, width), F32)],
        compiler_params=pltpu.CompilerParams(vmem_limit_bytes=VMEM_LIMIT),
    )(*own, *other, gain.reshape(1, width))


def body(n, tokens, gate_act, up_act, down_weight, norm_gain):
    half = down_weight.shape[1] // 2
    spans = spans_of(half)
    first, hidden = project(n, spans[:1], False, True, (gate_act, up_act), tokens, down_weight)
    sent = [first, *project(n, spans[1:], False, False, (hidden,), tokens, down_weight)]
    kept = project(n, spans, True, False, (hidden,), tokens, down_weight)

    def swap(x, bit):
        return lax.ppermute(x, "tensor", [(i, i ^ bit) for i in range(n)])

    def add(a, b):
        return (a.astype(F32) + b.astype(F32)).astype(BF16)

    arrived = [swap(x, 1) for x in sent]
    sums = [add(a, b) for a, b in zip(kept, arrived)]
    bit = 2
    while bit < n:
        sums = [add(x, swap(x, bit)) for x in sums]
        bit *= 2
    others = [swap(x, 1) for x in sums]
    residual_out, next_rows, next_scale = norm(tokens.shape[0], spans, sums, others, norm_gain)
    return residual_out, next_rows, next_scale


def solution(mesh):
    n = mesh.shape["tensor"]
    return jax.shard_map(
        lambda *args: body(n, *args),
        mesh=mesh,
        in_specs=(
            P(("dp", "tensor"), None),
            P("dp", "tensor"),
            P("dp", "tensor"),
            P("tensor", None),
            P(),
        ),
        out_specs=(P(("dp", "tensor"), None), P("dp", None), P("dp")),
        check_vma=False,
    )
```

```python
import functools

import jax
import jax.numpy as jnp
from jax import lax
from jax.experimental import pallas as pl
from jax.experimental.pallas import tpu as pltpu
from jax.sharding import PartitionSpec as P

F32, BF16 = jnp.float32, jnp.bfloat16
TILE = 512
CHUNKS = ((7, 2, True), (9, 1, True))
PLAN = (((0, False), (1, False)), ((0, True), (1, True)))
AFTER = {}
VMEM_LIMIT = 32 * 1024 * 1024


def chunks_of(n, width):
    whole, at, chunks = sum(share for share, _, _ in CHUNKS), 0, []
    for share, first, halved in CHUNKS:
        first = min(first, n // 2)
        bits = [1 << i for i in range(n.bit_length() - 1)]
        bits = [first, *(bit for bit in bits if bit != first)]
        wide = width * share // whole // 256 * 256
        if len(chunks) == len(CHUNKS) - 1:
            wide = width - at
        chunks.append((bits, halved, at, wide // 2 if halved else wide))
        at += wide
    return chunks


def side_of(me, bit):
    return lax.rem(lax.div(me, bit), 2)


def tiles_of(blocks):
    tiles = []
    for i, (*_, width, _) in enumerate(blocks):
        count = -(-width // TILE)
        piece = -(-width // count // 128) * 128
        tiles += [(i, c, min(piece, width - c)) for c in range(0, width, piece)]
    return tiles


def project_kernel(n, blocks, gated, waited, *refs):
    k = len(blocks)
    refs = refs[waited:]
    tiles = tiles_of(blocks)
    if gated:
        gate_hbm, up_hbm, tokens_hbm, weight_ref, *refs = refs
    else:
        hidden_ref, tokens_hbm, weight_ref, *refs = refs
    outs, refs = refs[:k], refs[k:]
    if gated:
        hidden_ref, gate_ref, up_ref, *refs = refs
    tokens_ref, *buffers, sem = refs
    me = lax.axis_index("tensor")

    def fetch(source, target, i):
        copy = pltpu.make_async_copy(source, target, sem.at[i])
        copy.start()
        return copy

    def columns(i, c, width):
        bits, halved, at, block, keep = blocks[i]
        if halved:
            side = side_of(me, bits[0])
            at += (side if keep else 1 - side) * block
        return pl.ds(pl.multiple_of(at + c, 128), width)

    if gated:
        gating = [fetch(gate_hbm, gate_ref, 1), fetch(up_hbm, up_ref, 2)]
    copies = []
    for j, tile in enumerate(tiles):
        copies.append(fetch(weight_ref.at[:, columns(*tile)], buffers[j], 3 + j))
        if j == 0:
            adding = fetch(tokens_hbm, tokens_ref, 0)
    if gated:
        for copy in gating:
            copy.wait()
        gate = gate_ref[...].astype(F32)
        hidden_ref[...] = (gate / (1.0 + jnp.exp(-gate)) * up_ref[...].astype(F32)).astype(BF16)
    rows = tokens_ref.shape[0]
    adding.wait()
    for j, tile in enumerate(tiles):
        i, c, width = tile
        own = jnp.concatenate([tokens_ref[:, columns(*tile)].astype(F32)] * n, axis=0)
        owner = lax.broadcasted_iota(jnp.int32, own.shape, 0) // rows
        copies[j].wait()
        product = jnp.dot(hidden_ref[...], buffers[j][...], preferred_element_type=F32)
        outs[i][:, c : c + width] = (product + jnp.where(owner == me, own, 0.0)).astype(BF16)


def project(n, blocks, gated, ins, tokens, weight, after=()):
    depth = weight.shape[0]
    rows = tokens.shape[0] * n
    vmem, hbm = pl.BlockSpec(memory_space=pltpu.VMEM), pl.BlockSpec(memory_space=pl.ANY)
    shapes = [jax.ShapeDtypeStruct((rows, w), BF16) for *_, w, _ in blocks]
    scratch = [pltpu.VMEM(tokens.shape, BF16)]
    if gated:
        shapes.append(jax.ShapeDtypeStruct((rows, depth), BF16))
        scratch = [pltpu.VMEM((rows, depth), BF16)] * 2 + scratch
    columns = sum(w for *_, w, _ in blocks)
    tiles = tiles_of(blocks)
    pinned = [*(ins if gated else ()), tokens, weight]
    pinned = [pltpu.with_memory_space_constraint(x, pltpu.HBM) for x in pinned]
    return pl.pallas_call(
        functools.partial(project_kernel, n, blocks, gated, len(after)),
        out_shape=shapes,
        in_specs=[hbm] * len(after) + [hbm if gated else vmem] * len(ins) + [hbm, hbm],
        out_specs=[vmem] * len(shapes),
        scratch_shapes=scratch
        + [pltpu.VMEM((depth, w), BF16) for _, _, w in tiles]
        + [pltpu.SemaphoreType.DMA((len(tiles) + 3,))],
        compiler_params=pltpu.CompilerParams(vmem_limit_bytes=VMEM_LIMIT),
        cost_estimate=pl.CostEstimate(
            flops=2 * rows * depth * columns,
            bytes_accessed=2 * depth * columns,
            transcendentals=0,
        ),
    )(*after, *(() if gated else ins), *pinned)


def norm_kernel(chunks, *refs):
    *pieces, gain_ref, residual_ref, rows_ref, scale_ref, scaled_ref = refs
    me = lax.axis_index("tensor")
    mine = pl.ds(pl.multiple_of(me * residual_ref.shape[0], 16), residual_ref.shape[0])
    squares, largest = 0.0, 0.0
    pieces = iter(pieces)
    for bits, halved, at, width in chunks:
        side = side_of(me, bits[0])
        for first in (at + side * width, at + (1 - side) * width) if halved else (at,):
            piece = next(pieces)
            cols = pl.ds(pl.multiple_of(first, 128), width)
            residual_ref[:, cols] = piece[mine, :]
            residual = piece[...].astype(F32)
            scaled = residual * gain_ref[:, cols]
            scaled_ref[:, cols] = scaled
            squares += jnp.sum(residual * residual, axis=1, keepdims=True)
            largest = jnp.maximum(largest, jnp.max(jnp.abs(scaled), axis=1, keepdims=True))
    rows_ref[...] = (scaled_ref[...] * (1.0 / largest)).astype(BF16)
    mean = squares * (1.0 / rows_ref.shape[1])
    scale_ref[...] = (largest * lax.rsqrt(mean + 1e-05)).reshape(-1)


def norm(rows, chunks, pieces, gain):
    count, width = pieces[0].shape[0], gain.shape[0]
    vmem = pl.BlockSpec(memory_space=pltpu.VMEM)
    return pl.pallas_call(
        functools.partial(norm_kernel, chunks),
        out_shape=[
            jax.ShapeDtypeStruct((rows, width), BF16),
            jax.ShapeDtypeStruct((count, width), BF16),
            jax.ShapeDtypeStruct((count,), F32),
        ],
        in_specs=[vmem] * (len(pieces) + 1),
        out_specs=[vmem] * 3,
        scratch_shapes=[pltpu.VMEM((count, width), F32)],
        compiler_params=pltpu.CompilerParams(vmem_limit_bytes=VMEM_LIMIT),
    )(*pieces, gain.reshape(1, width))


def body(n, tokens, gate_act, up_act, down_weight, norm_gain):
    chunks = chunks_of(n, down_weight.shape[1])
    def swap(x, bit):
        return lax.ppermute(x, "tensor", [(i, i ^ bit) for i in range(n)])

    def add(a, b):
        return (a.astype(F32) + b.astype(F32)).astype(BF16)

    made, arrived = {}, {}
    for step, chosen in enumerate(PLAN):
        ins = (hidden,) if step else (gate_act, up_act)
        blocks = [(*chunks[i], keep) for i, keep in chosen]
        after = [arrived[AFTER[step]]] if step in AFTER else []
        outs = project(n, blocks, not step, ins, tokens, down_weight, after)
        if not step:
            *outs, hidden = outs
        made.update(zip(chosen, outs))
        for i, keep in chosen:
            bits, halved, _, _ = chunks[i]
            if not keep or not halved:
                arrived[i] = swap(made[i, keep], bits[0])

    pieces = []
    for i, (bits, halved, _, _) in enumerate(chunks):
        total = add(made[i, True], arrived[i])
        for bit in bits[1:]:
            total = add(total, swap(total, bit))
        pieces.append(total)
        if halved:
            pieces.append(swap(total, bits[0]))
    return norm(tokens.shape[0], chunks, pieces, norm_gain)


def solution(mesh):
    n = mesh.shape["tensor"]
    return jax.shard_map(
        lambda *args: body(n, *args),
        mesh=mesh,
        in_specs=(
            P(("dp", "tensor"), None),
            P("dp", "tensor"),
            P("dp", "tensor"),
            P("tensor", None),
            P(),
        ),
        out_specs=(P(("dp", "tensor"), None), P("dp", None), P("dp")),
        check_vma=False,
    )
```

```python
import functools

import jax
import jax.numpy as jnp
from jax import lax
from jax.experimental import pallas as pl
from jax.experimental.pallas import tpu as pltpu
from jax.sharding import PartitionSpec as P

F32, BF16 = jnp.float32, jnp.bfloat16
TILE = 512
CHUNKS = ((8, ((2, 1), (1, 2))), (8, ((1, 2), (1, 3))))
PLAN = (((0, False), (1, False)), ((0, True), (1, True)))
VMEM_LIMIT = 32 * 1024 * 1024


def chunks_of(n, width):
    whole, at, chunks = sum(share for share, _ in CHUNKS), 0, []
    for share, firsts in CHUNKS:
        rest = [1 << i for i in range(2, n.bit_length() - 1)]
        masks = [[*first, *rest] if n > 2 else [1] for first in firsts]
        wide = width * share // whole // 256 * 256
        if len(chunks) == len(CHUNKS) - 1:
            wide = width - at
        chunks.append((masks, at, wide // 2))
        at += wide
    return chunks


def parity(number):
    return number.bit_count() % 2


def side_of(n, masks):
    me, core = lax.axis_index("tensor"), lax.rem(lax.axis_index("dp"), 2)
    sides = []
    for first, *later in masks:
        marks = [m for m in range(n) if parity(m & first) and not any(parity(m & x) for x in later)]
        bits = [lax.rem(lax.div(me, 1 << i), 2) for i in range(n.bit_length()) if marks[0] >> i & 1]
        sides.append(lax.rem(sum(bits), 2))
    return jnp.where(core == 0, sides[0], sides[1])


def tiles_of(blocks):
    tiles = []
    for i, (_, _, width, _) in enumerate(blocks):
        count = -(-width // TILE)
        piece = -(-width // count // 128) * 128
        tiles += [(i, c, min(piece, width - c)) for c in range(0, width, piece)]
    return tiles


def project_kernel(n, blocks, gated, *refs):
    k = len(blocks)
    tiles = tiles_of(blocks)
    if gated:
        gate_hbm, up_hbm, tokens_hbm, weight_ref, *refs = refs
    else:
        hidden_ref, tokens_hbm, weight_ref, *refs = refs
    outs, refs = refs[:k], refs[k:]
    if gated:
        hidden_ref, gate_ref, up_ref, *refs = refs
    tokens_ref, *buffers, sem = refs
    me = lax.axis_index("tensor")

    def fetch(source, target, i):
        copy = pltpu.make_async_copy(source, target, sem.at[i])
        copy.start()
        return copy

    def columns(i, c, width):
        masks, at, block, keep = blocks[i]
        side = side_of(n, masks)
        at += (side if keep else 1 - side) * block
        return pl.ds(pl.multiple_of(at + c, 128), width)

    if gated:
        gating = [fetch(gate_hbm, gate_ref, 1), fetch(up_hbm, up_ref, 2)]
    copies = []
    for j, tile in enumerate(tiles):
        copies.append(fetch(weight_ref.at[:, columns(*tile)], buffers[j], 3 + j))
        if j == 0:
            adding = fetch(tokens_hbm, tokens_ref, 0)
    if gated:
        for copy in gating:
            copy.wait()
        gate = gate_ref[...].astype(F32)
        hidden_ref[...] = (gate / (1.0 + jnp.exp(-gate)) * up_ref[...].astype(F32)).astype(BF16)
    rows = tokens_ref.shape[0]
    adding.wait()
    for j, tile in enumerate(tiles):
        i, c, width = tile
        own = jnp.concatenate([tokens_ref[:, columns(*tile)].astype(F32)] * n, axis=0)
        owner = lax.broadcasted_iota(jnp.int32, own.shape, 0) // rows
        copies[j].wait()
        product = jnp.dot(hidden_ref[...], buffers[j][...], preferred_element_type=F32)
        outs[i][:, c : c + width] = (product + jnp.where(owner == me, own, 0.0)).astype(BF16)


def project(n, blocks, gated, ins, tokens, weight):
    depth = weight.shape[0]
    rows = tokens.shape[0] * n
    vmem, hbm = pl.BlockSpec(memory_space=pltpu.VMEM), pl.BlockSpec(memory_space=pl.ANY)
    shapes = [jax.ShapeDtypeStruct((rows, w), BF16) for *_, w, _ in blocks]
    scratch = [pltpu.VMEM(tokens.shape, BF16)]
    if gated:
        shapes.append(jax.ShapeDtypeStruct((rows, depth), BF16))
        scratch = [pltpu.VMEM((rows, depth), BF16)] * 2 + scratch
    columns = sum(w for *_, w, _ in blocks)
    tiles = tiles_of(blocks)
    pinned = [*(ins if gated else ()), tokens, weight]
    pinned = [pltpu.with_memory_space_constraint(x, pltpu.HBM) for x in pinned]
    return pl.pallas_call(
        functools.partial(project_kernel, n, blocks, gated),
        out_shape=shapes,
        in_specs=[hbm if gated else vmem] * len(ins) + [hbm, hbm],
        out_specs=[vmem] * len(shapes),
        scratch_shapes=scratch
        + [pltpu.VMEM((depth, w), BF16) for _, _, w in tiles]
        + [pltpu.SemaphoreType.DMA((len(tiles) + 3,))],
        compiler_params=pltpu.CompilerParams(vmem_limit_bytes=VMEM_LIMIT),
        cost_estimate=pl.CostEstimate(
            flops=2 * rows * depth * columns,
            bytes_accessed=2 * depth * columns,
            transcendentals=0,
        ),
    )(*(() if gated else ins), *pinned)


def norm_kernel(n, chunks, *refs):
    *pieces, gain_ref, residual_ref, rows_ref, scale_ref, scaled_ref = refs
    me = lax.axis_index("tensor")
    mine = pl.ds(pl.multiple_of(me * residual_ref.shape[0], 16), residual_ref.shape[0])
    squares, largest = 0.0, 0.0
    pieces = iter(pieces)
    for masks, at, width in chunks:
        side = side_of(n, masks)
        for first in (at + side * width, at + (1 - side) * width):
            piece = next(pieces)
            cols = pl.ds(pl.multiple_of(first, 128), width)
            residual_ref[:, cols] = piece[mine, :]
            residual = piece[...].astype(F32)
            scaled = residual * gain_ref[:, cols]
            scaled_ref[:, cols] = scaled
            squares += jnp.sum(residual * residual, axis=1, keepdims=True)
            largest = jnp.maximum(largest, jnp.max(jnp.abs(scaled), axis=1, keepdims=True))
    rows_ref[...] = (scaled_ref[...] * (1.0 / largest)).astype(BF16)
    mean = squares * (1.0 / rows_ref.shape[1])
    scale_ref[...] = (largest * lax.rsqrt(mean + 1e-05)).reshape(-1)


def norm(n, rows, chunks, pieces, gain):
    count, width = pieces[0].shape[0], gain.shape[0]
    vmem = pl.BlockSpec(memory_space=pltpu.VMEM)
    return pl.pallas_call(
        functools.partial(norm_kernel, n, chunks),
        out_shape=[
            jax.ShapeDtypeStruct((rows, width), BF16),
            jax.ShapeDtypeStruct((count, width), BF16),
            jax.ShapeDtypeStruct((count,), F32),
        ],
        in_specs=[vmem] * (len(pieces) + 1),
        out_specs=[vmem] * 3,
        scratch_shapes=[pltpu.VMEM((count, width), F32)],
        compiler_params=pltpu.CompilerParams(vmem_limit_bytes=VMEM_LIMIT),
    )(*pieces, gain.reshape(1, width))


def body(n, batches, tokens, gate_act, up_act, down_weight, norm_gain):
    chunks = chunks_of(n, down_weight.shape[1])

    def swap(x, masks):
        pairs = [
            (d * n + t, d * n + (t ^ masks[d % 2])) for d in range(batches) for t in range(n)
        ]
        return lax.ppermute(x, ("dp", "tensor"), pairs)

    def add(a, b):
        return (a.astype(F32) + b.astype(F32)).astype(BF16)

    stages = len(chunks[0][0][0]) + 1
    made, arrivals, sums = {}, {}, {}

    def run(step):
        ins = (made["hidden"],) if step else (gate_act, up_act)
        blocks = [(*chunks[i], keep) for i, keep in PLAN[step]]
        return project(n, blocks, not step, ins, tokens, down_weight)

    def block(i, keep):
        if not made:
            *outs, made["hidden"] = run(0)
            made.update(zip(PLAN[0], outs))
        if (i, keep) not in made:
            step = [(i, keep) in chosen for chosen in PLAN].index(True)
            made.update(zip(PLAN[step], run(step)))
        return made[i, keep]

    def arrived(i, stage):
        if (i, stage) not in arrivals:
            x = total(i, stage - 1) if stage else block(i, False)
            masks = [[*masks, masks[0]][stage] for masks in chunks[i][0]]
            arrivals[i, stage] = swap(x, masks)
        return arrivals[i, stage]

    def total(i, stage):
        if (i, stage) not in sums:
            other = arrived(i, stage)
            sums[i, stage] = add(total(i, stage - 1) if stage else block(i, True), other)
        return sums[i, stage]

    pieces = []
    for i in range(len(chunks)):
        pieces += [total(i, stages - 2), arrived(i, stages - 1)]
    return norm(n, tokens.shape[0], chunks, pieces, norm_gain)


def solution(mesh):
    n = mesh.shape["tensor"]
    return jax.shard_map(
        lambda *args: body(n, mesh.shape["dp"], *args),
        mesh=mesh,
        in_specs=(
            P(("dp", "tensor"), None),
            P("dp", "tensor"),
            P("dp", "tensor"),
            P("tensor", None),
            P(),
        ),
        out_specs=(P(("dp", "tensor"), None), P("dp", None), P("dp")),
        check_vma=False,
    )
```

```python
import functools

import jax
import jax.numpy as jnp
from jax import lax
from jax.experimental import pallas as pl
from jax.experimental.pallas import tpu as pltpu
from jax.sharding import PartitionSpec as P

F32, BF16 = jnp.float32, jnp.bfloat16
TILES = {True: 512, False: 1024}
CHUNKS = ((8, ((2, 1), (1, 2))), (8, ((1, 2), (1, 3))))
PLAN = (((0, False), (1, False)), ((0, True), (1, True)))
VMEM_LIMIT = 32 * 1024 * 1024


def chunks_of(n, width):
    whole, at, chunks = sum(share for share, _ in CHUNKS), 0, []
    for share, firsts in CHUNKS:
        rest = [1 << i for i in range(2, n.bit_length() - 1)]
        masks = [[*first, *rest] if n > 2 else [1] for first in firsts]
        wide = width * share // whole // 256 * 256
        if len(chunks) == len(CHUNKS) - 1:
            wide = width - at
        chunks.append((masks, at, wide // 2))
        at += wide
    return chunks


def parity(number):
    return number.bit_count() % 2


def side_of(n, masks):
    me, core = lax.axis_index("tensor"), lax.rem(lax.axis_index("dp"), 2)
    sides = []
    for first, *later in masks:
        marks = [m for m in range(n) if parity(m & first) and not any(parity(m & x) for x in later)]
        bits = [lax.rem(lax.div(me, 1 << i), 2) for i in range(n.bit_length()) if marks[0] >> i & 1]
        sides.append(lax.rem(sum(bits), 2))
    return jnp.where(core == 0, sides[0], sides[1])


def tiles_of(blocks, most):
    tiles = []
    for i, (_, _, width, _) in enumerate(blocks):
        count = -(-width // most)
        piece = -(-width // count // 128) * 128
        tiles += [(i, c, min(piece, width - c)) for c in range(0, width, piece)]
    return tiles


def project_kernel(n, blocks, gated, *refs):
    k = len(blocks)
    tiles = tiles_of(blocks, TILES[gated])
    if gated:
        gate_hbm, up_hbm, tokens_hbm, weight_ref, *refs = refs
    else:
        hidden_ref, tokens_hbm, weight_ref, *refs = refs
    outs, refs = refs[:k], refs[k:]
    if gated:
        hidden_ref, gate_ref, up_ref, *refs = refs
    tokens_ref, *buffers, sem = refs
    me = lax.axis_index("tensor")

    def fetch(source, target, i):
        copy = pltpu.make_async_copy(source, target, sem.at[i])
        copy.start()
        return copy

    def columns(i, c, width):
        masks, at, block, keep = blocks[i]
        side = side_of(n, masks)
        at += (side if keep else 1 - side) * block
        return pl.ds(pl.multiple_of(at + c, 128), width)

    if gated:
        gating = [fetch(gate_hbm, gate_ref, 1), fetch(up_hbm, up_ref, 2)]
    copies = []
    for j, tile in enumerate(tiles):
        copies.append(fetch(weight_ref.at[:, columns(*tile)], buffers[j], 3 + j))
        if j == 0:
            adding = fetch(tokens_hbm, tokens_ref, 0)
    if gated:
        for copy in gating:
            copy.wait()
        gate = gate_ref[...].astype(F32)
        hidden_ref[...] = (gate / (1.0 + jnp.exp(-gate)) * up_ref[...].astype(F32)).astype(BF16)
    rows = tokens_ref.shape[0]
    adding.wait()
    for j, tile in enumerate(tiles):
        i, c, width = tile
        own = jnp.concatenate([tokens_ref[:, columns(*tile)].astype(F32)] * n, axis=0)
        owner = lax.broadcasted_iota(jnp.int32, own.shape, 0) // rows
        copies[j].wait()
        product = jnp.dot(hidden_ref[...], buffers[j][...], preferred_element_type=F32)
        outs[i][:, c : c + width] = (product + jnp.where(owner == me, own, 0.0)).astype(BF16)


def project(n, blocks, gated, ins, tokens, weight):
    depth = weight.shape[0]
    rows = tokens.shape[0] * n
    vmem, hbm = pl.BlockSpec(memory_space=pltpu.VMEM), pl.BlockSpec(memory_space=pl.ANY)
    shapes = [jax.ShapeDtypeStruct((rows, w), BF16) for *_, w, _ in blocks]
    scratch = [pltpu.VMEM(tokens.shape, BF16)]
    if gated:
        shapes.append(jax.ShapeDtypeStruct((rows, depth), BF16))
        scratch = [pltpu.VMEM((rows, depth), BF16)] * 2 + scratch
    columns = sum(w for *_, w, _ in blocks)
    tiles = tiles_of(blocks, TILES[gated])
    pinned = [*(ins if gated else ()), tokens, weight]
    pinned = [pltpu.with_memory_space_constraint(x, pltpu.HBM) for x in pinned]
    return pl.pallas_call(
        functools.partial(project_kernel, n, blocks, gated),
        out_shape=shapes,
        in_specs=[hbm if gated else vmem] * len(ins) + [hbm, hbm],
        out_specs=[vmem] * len(shapes),
        scratch_shapes=scratch
        + [pltpu.VMEM((depth, w), BF16) for _, _, w in tiles]
        + [pltpu.SemaphoreType.DMA((len(tiles) + 3,))],
        compiler_params=pltpu.CompilerParams(vmem_limit_bytes=VMEM_LIMIT),
        cost_estimate=pl.CostEstimate(
            flops=2 * rows * depth * columns,
            bytes_accessed=2 * depth * columns,
            transcendentals=0,
        ),
    )(*(() if gated else ins), *pinned)


def norm_kernel(n, chunks, *refs):
    *pieces, gain_ref, residual_ref, rows_ref, scale_ref, scaled_ref = refs
    me = lax.axis_index("tensor")
    mine = pl.ds(pl.multiple_of(me * residual_ref.shape[0], 16), residual_ref.shape[0])
    squares, largest = 0.0, 0.0
    pieces = iter(pieces)
    for masks, at, width in chunks:
        side = side_of(n, masks)
        for first in (at + side * width, at + (1 - side) * width):
            piece = next(pieces)
            cols = pl.ds(pl.multiple_of(first, 128), width)
            residual_ref[:, cols] = piece[mine, :]
            residual = piece[...].astype(F32)
            scaled = residual * gain_ref[:, cols]
            scaled_ref[:, cols] = scaled
            squares += jnp.sum(residual * residual, axis=1, keepdims=True)
            largest = jnp.maximum(largest, jnp.max(jnp.abs(scaled), axis=1, keepdims=True))
    rows_ref[...] = (scaled_ref[...] * (1.0 / largest)).astype(BF16)
    mean = squares * (1.0 / rows_ref.shape[1])
    scale_ref[...] = (largest * lax.rsqrt(mean + 1e-05)).reshape(-1)


def norm(n, rows, chunks, pieces, gain):
    count, width = pieces[0].shape[0], gain.shape[0]
    vmem = pl.BlockSpec(memory_space=pltpu.VMEM)
    return pl.pallas_call(
        functools.partial(norm_kernel, n, chunks),
        out_shape=[
            jax.ShapeDtypeStruct((rows, width), BF16),
            jax.ShapeDtypeStruct((count, width), BF16),
            jax.ShapeDtypeStruct((count,), F32),
        ],
        in_specs=[vmem] * (len(pieces) + 1),
        out_specs=[vmem] * 3,
        scratch_shapes=[pltpu.VMEM((count, width), F32)],
        compiler_params=pltpu.CompilerParams(vmem_limit_bytes=VMEM_LIMIT),
    )(*pieces, gain.reshape(1, width))


def body(n, batches, tokens, gate_act, up_act, down_weight, norm_gain):
    chunks = chunks_of(n, down_weight.shape[1])

    def swap(x, masks):
        pairs = [
            (d * n + t, d * n + (t ^ masks[d % 2])) for d in range(batches) for t in range(n)
        ]
        return lax.ppermute(x, ("dp", "tensor"), pairs)

    def add(a, b):
        return (a.astype(F32) + b.astype(F32)).astype(BF16)

    stages = len(chunks[0][0][0]) + 1
    made, arrivals, sums = {}, {}, {}

    def run(step):
        ins = (made["hidden"],) if step else (gate_act, up_act)
        blocks = [(*chunks[i], keep) for i, keep in PLAN[step]]
        return project(n, blocks, not step, ins, tokens, down_weight)

    def block(i, keep):
        if not made:
            *outs, made["hidden"] = run(0)
            made.update(zip(PLAN[0], outs))
        if (i, keep) not in made:
            step = [(i, keep) in chosen for chosen in PLAN].index(True)
            made.update(zip(PLAN[step], run(step)))
        return made[i, keep]

    def arrived(i, stage):
        if (i, stage) not in arrivals:
            x = total(i, stage - 1) if stage else block(i, False)
            masks = [[*masks, masks[0]][stage] for masks in chunks[i][0]]
            arrivals[i, stage] = swap(x, masks)
        return arrivals[i, stage]

    def total(i, stage):
        if (i, stage) not in sums:
            other = arrived(i, stage)
            sums[i, stage] = add(total(i, stage - 1) if stage else block(i, True), other)
        return sums[i, stage]

    pieces = []
    for i in range(len(chunks)):
        pieces += [total(i, stages - 2), arrived(i, stages - 1)]
    return norm(n, tokens.shape[0], chunks, pieces, norm_gain)


def solution(mesh):
    n = mesh.shape["tensor"]
    return jax.shard_map(
        lambda *args: body(n, mesh.shape["dp"], *args),
        mesh=mesh,
        in_specs=(
            P(("dp", "tensor"), None),
            P("dp", "tensor"),
            P("dp", "tensor"),
            P("tensor", None),
            P(),
        ),
        out_specs=(P(("dp", "tensor"), None), P("dp", None), P("dp")),
        check_vma=False,
    )
```
